32 devices in a mesh: sec: 4 (over y, x), term: 8 (over z, core).
Axes of the slice: x: 2, y: 2, z: 4, core: 2. Of those that a mesh axis runs over, the one named last changes fastest.
Arguments:
- psi: bfloat16 [8, 2, 512, 512], P('sec'), may hold values from -6 to 6
- left_ops: bfloat16 [8, 8, 512, 512], P('term', 'sec'), may hold values from -0.25 to 0.25
- right_ops: bfloat16 [8, 8, 512, 512], P('term', 'sec'), may hold values from -0.09375 to 0.09375
- shift: int32 [8], P('term'), may hold values from -2 to 2, as said below
- live: int32 [8], P('term'), may hold values 0 or 1
Outputs:
- sigma: bfloat16 [8, 2, 512, 512], P('sec', None, 'term')
The draws below stay inside these ranges and needn't reach their ends.
Inputs may be any that keep to these rules, and one draw needn't show every extreme that they name: `shift`: every draw holds both -2 and 2.
All inputs are finite; a program needn't handle non-finite values. No bound on the sum of `live` on one device may be relied on, other than what follows from the above.
Results may differ from the reference program's by a relative error of at most 0.0049.
Values may be sent and summed in bfloat16 or wider, within the bound.
No kernel may reach another device: no remote copies, remote signals or barrier semaphores. Data moves between devices by JAX's collectives and lax.ppermute only.
A program may use at most 64 MiB of HBM per device.

```python
import jax
import jax.numpy as jnp
from jax import lax

B = 512
V = 2
DQ = 2
NSEC = 8
TERMS = 8


def draw_shift(key, part):
    values = jax.random.randint(key, (TERMS,), -DQ, DQ + 1, dtype=jnp.int32)
    return values.at[0].set(-DQ).at[1].set(DQ)


def touch_ends(result, own_key, least, high):
    longest = result.shape.index(max(result.shape))
    spots = []
    for shift in (0, 1):
        where = [jax.random.randint(jax.random.fold_in(own_key, axis), (), 0, length) for axis, length in enumerate(result.shape)]
        where[longest] = (where[longest] + shift) % result.shape[longest]
        spots.append(tuple(where))
    return result.at[spots[0]].set(least).at[spots[1]].set(high)


def block_levels(stream_key, extent, shards, low, high):
    factor_of = 1.0
    for position, blocks in shards:
        draws = jax.random.uniform(jax.random.fold_in(jax.random.fold_in(stream_key, 6), position), (blocks,), jnp.float32, low / len(shards), high / len(shards))
        factor_of = factor_of * jnp.repeat(jnp.exp(draws), extent[position] // blocks).reshape((-1,) + (1,) * (len(extent) - 1 - position))
    return factor_of


def gaussian(stream_key, extent, deviation, most, shards=(), kind=jnp.bfloat16):
    factor_of = block_levels(stream_key, extent, shards, -0.22, 0.18) if shards else 1.0
    entries = jax.random.normal(stream_key, extent, jnp.float32) * deviation * factor_of
    return jnp.minimum(jnp.maximum(entries, -most), most).astype(kind)


def setup_inputs(seed: int = 0) -> dict:
    splits = jax.random.split(jax.random.key(seed), 6)
    return {
        "psi": gaussian(splits[0], (NSEC, V, B, B), 1.0, 6.0, ((0, 4),)),
        "left_ops": gaussian(splits[1], (TERMS, NSEC, B, B), B ** -0.5, 0.25, ((0, 8), (1, 4))),
        "right_ops": gaussian(splits[2], (TERMS, NSEC, B, B), (B * TERMS) ** -0.5, 0.09375, ((0, 8), (1, 4))),
        "shift": draw_shift(jax.random.fold_in(splits[5], 71), 0),
        "live": touch_ends((jax.random.randint(splits[4], (TERMS,), 0, 4) < 3).astype(jnp.int32), jax.random.fold_in(splits[4], 1), 0, 1),
    }


def reference(psi, left_ops, right_ops, shift, live):
    padded = jnp.pad(psi, ((DQ, DQ), (0, 0), (0, 0), (0, 0)))

    def one_term(acc, index):
        start = (DQ - shift[index]).astype(jnp.int32)
        block = lax.dynamic_slice_in_dim(padded, start, NSEC, 0)
        inner = jnp.einsum('sab,svbc->svac', left_ops[index].astype(jnp.float32), block.astype(jnp.float32)).astype(jnp.bfloat16)
        outer = jnp.einsum('svac,sdc->svad', inner.astype(jnp.float32), right_ops[index].astype(jnp.float32))
        return acc + outer * live[index].astype(jnp.float32), None

    start_acc = jnp.zeros((NSEC, V, B, B), jnp.float32)
    total, _ = lax.scan(one_term, start_acc, jnp.arange(TERMS, dtype=jnp.int32))
    return total.astype(jnp.bfloat16)
```

```python
import functools

import jax
import jax.numpy as jnp
from jax import lax
from jax.experimental import pallas as pl
from jax.experimental.pallas import tpu as pltpu
from jax.sharding import PartitionSpec as P

DQ = 2
HALVES = 2


def piece_kernel(first_slot, slots, meta, *refs):
    halo = refs[: slots * HALVES]
    psi, left0, right0, left1, right1, keep, send, src, left, right, total, sem = refs[slots * HALVES :]
    rows = src.shape[1] // HALVES
    sector, core, bit = meta[0], meta[1], meta[2]

    def operand_copies(term):
        pair = ((left0, right0), (left1, right1))[term]
        return (
            pltpu.make_async_copy(pair[0].at[0, sector], left.at[term], sem.at[term, HALVES]),
            pltpu.make_async_copy(pair[1].at[0, sector], right.at[term], sem.at[term, HALVES + 1]),
        )

    def source_copy(term, ref, half):
        return pltpu.make_async_copy(ref, src.at[term, pl.ds(half * rows, rows)], sem.at[term, half])

    for term in range(2):
        slot = meta[3 + term]
        for k in range(slots):
            @pl.when(slot == k)
            def _(k=k, term=term):
                for half in range(HALVES):
                    source_copy(term, halo[k * HALVES + half], half).start()
        for own in range(2):
            @pl.when(slot == slots + own)
            def _(own=own, term=term):
                for half in range(HALVES):
                    part = psi.at[own, core, pl.ds(half * rows, rows)]
                    source_copy(term, part, half).start()
        for copy in operand_copies(term):
            copy.start()

    for term in range(2):
        for half in range(HALVES):
            source_copy(term, psi.at[0, 0, pl.ds(0, rows)], half).wait()
        for copy in operand_copies(term):
            copy.wait()
        weight = meta[5 + term].astype(jnp.float32)
        for half in range(2):
            part = pl.ds(half * (left.shape[1] // 2), left.shape[1] // 2)
            inner = jnp.dot(left[term, part], src[term], preferred_element_type=jnp.float32).astype(jnp.bfloat16)
            outer = lax.dot_general(
                inner, right[term], (((1,), (1,)), ((), ())), preferred_element_type=jnp.float32
            ) * weight
            if term == 0:
                total[part] = outer
            else:
                total[part] += outer

    count, height = keep.shape[0], keep.shape[1]
    for k in range(count):
        at = pl.multiple_of((2 * k + bit) * height, height)
        keep[k] = total[pl.ds(at, height)].astype(keep.dtype)
        at = pl.multiple_of((2 * k + 1 - bit) * height, height)
        send[k] = total[pl.ds(at, height)].astype(send.dtype)


def piece(meta, halo, psi, left0, right0, left1, right1, chips):
    size = psi.shape[-1]
    slots = len(halo)
    flat = [part for block in halo for part in block]
    out = (chips // 2, size // chips, size)
    anywhere = pl.BlockSpec(memory_space=pl.ANY)
    return pl.pallas_call(
        functools.partial(piece_kernel, 0, slots),
        out_shape=(jax.ShapeDtypeStruct(out, jnp.float32), jax.ShapeDtypeStruct(out, jnp.bfloat16)),
        in_specs=[pl.BlockSpec(memory_space=pltpu.SMEM)] + [anywhere] * (len(flat) + 5),
        out_specs=(pl.BlockSpec(memory_space=pltpu.VMEM),) * 2,
        scratch_shapes=[
            pltpu.VMEM((2, size, size), jnp.bfloat16),
            pltpu.VMEM((2, size, size), jnp.bfloat16),
            pltpu.VMEM((2, size, size), jnp.bfloat16),
            pltpu.VMEM((size, size), jnp.float32),
            pltpu.SemaphoreType.DMA((2, HALVES + 2)),
        ],
        compiler_params=pltpu.CompilerParams(vmem_limit_bytes=16 * 1024 * 1024),
        cost_estimate=pl.CostEstimate(flops=8 * size**3, bytes_accessed=10 * size * size, transcendentals=0),
        name="piece",
    )(meta, *flat, psi, left0, right0, left1, right1)


def halving(keep, send, z, rounds):
    for step in range(rounds):
        pairs = [(d, d ^ (2 << step)) for d in range(lax.axis_size("term"))]
        got = lax.ppermute(send, "term", pairs)
        total = keep + got.astype(jnp.float32)
        if step == rounds - 1:
            return total[0]
        total = total.reshape(total.shape[0] // 2, 2, *total.shape[1:])
        bit = (z >> (step + 1)) & 1
        keep = lax.dynamic_index_in_dim(total, bit, 1, False)
        send = lax.dynamic_index_in_dim(total, 1 - bit, 1, False).astype(jnp.bfloat16)


def local(psi, left_ops, right_ops, shift, live):
    secs, terms = lax.axis_size("sec"), lax.axis_size("term")
    chips = terms // 2
    rounds = chips.bit_length() - 1
    size = psi.shape[-1]
    i, term = lax.axis_index("sec"), lax.axis_index("term")
    core, z = term % 2, term // 2
    odd = i % 2
    cores = [(d, d ^ 1) for d in range(terms)]
    xswap = [(d, d ^ 1) for d in range(secs)]

    mine = lax.dynamic_index_in_dim(psi, core, 1, False)
    order = (lax.dynamic_index_in_dim(mine, odd, 0, False), lax.dynamic_index_in_dim(mine, 1 - odd, 0, False))
    parts = [jnp.split(block, HALVES, axis=0) for block in order]
    near = [[lax.ppermute(p, "sec", xswap) for p in block] for block in parts]
    left1 = lax.ppermute(left_ops, "term", cores)
    right1 = lax.ppermute(right_ops, "term", cores)
    other = lax.ppermute(jnp.concatenate([shift, live]), "term", cores)
    if secs == 4:
        yswap = [(d, d ^ 2) for d in range(secs)]
        far = [[lax.ppermute(p, "sec", yswap) for p in block] for block in near]
    else:
        nexts = [(d, d + 1) for d in range(1, secs - 1, 2)]
        nexts = nexts + [(b, a) for a, b in nexts]
        far = [[lax.ppermute(p, "sec", nexts) for p in block] for block in parts]

    shifts = jnp.stack([shift[0], other[0]])
    lives = jnp.stack([live[0], other[1]])
    sign = 2 * odd - 1
    outs = []
    for s in range(2):
        sector = jnp.where(odd == 1, s, 1 - s)
        rel = sector - shifts
        there = ((rel >= 0) | (i > 0)) & ((rel <= 1) | (i < secs - 1))
        place = s - sign * shifts
        if s == 0:
            halo = (near[0], near[1], far[0])
            slot = jnp.where(place == 2, 2, place + 2)
        else:
            halo = (near[1], far[0], far[1])
            slot = jnp.where(place >= 2, place - 1, place + 1)
        slot = jnp.where((rel == 0) | (rel == 1), 3 + rel, slot)
        weight = jnp.where(there, lives, 0)
        meta = jnp.concatenate([jnp.stack([sector, core, z % 2]), slot, weight]).astype(jnp.int32)
        keep, send = piece(meta, halo, psi, left_ops, right_ops, left1, right1, chips)
        total = halving(keep, send, z, rounds).reshape(2, size // terms, size)
        own = lax.dynamic_index_in_dim(total, core, 0, False).astype(jnp.bfloat16)
        off = lax.dynamic_index_in_dim(total, 1 - core, 0, False).astype(jnp.bfloat16)
        got = lax.ppermute(off, "term", cores)
        outs.append(jnp.where(core == 0, jnp.stack([own, got]), jnp.stack([got, own])))
    return jnp.where(odd == 1, jnp.stack(outs), jnp.stack(outs[::-1]))


def solution(mesh):
    in_specs = (
        P("sec", None, None, None),
        P("term", "sec", None, None),
        P("term", "sec", None, None),
        P("term"),
        P("term"),
    )
    out_specs = P("sec", None, "term", None)
    return jax.shard_map(local, mesh=mesh, in_specs=in_specs, out_specs=out_specs, check_vma=False)
```

```python
import jax
import jax.numpy as jnp
from jax import lax
from jax.experimental import pallas as pl
from jax.experimental.pallas import tpu as pltpu
from jax.sharding import PartitionSpec as P

DQ = 2
VMEM_LIMIT = 12 * 1024 * 1024
SMEM_SPEC = pl.BlockSpec(memory_space=pltpu.SMEM)
VMEM_SPEC = pl.BlockSpec(memory_space=pltpu.VMEM)
ANY_SPEC = pl.BlockSpec(memory_space=pl.ANY)


def in_vmem(array):
    return pltpu.with_memory_space_constraint(array, pltpu.VMEM)


def in_hbm(array):
    return pltpu.with_memory_space_constraint(array, pltpu.HBM)


def call(body, name, **kwargs):
    return pl.pallas_call(
        body,
        compiler_params=pltpu.CompilerParams(vmem_limit_bytes=VMEM_LIMIT),
        cost_estimate=pl.CostEstimate(flops=1000, bytes_accessed=1000, transcendentals=0),
        name=name,
        **kwargs,
    )


def cut(place, psi, left, right):
    size = psi.shape[-1]
    rows = size // 2

    def body(place_ref, psi_ref, left_ref, right_ref, *refs):
        parts, pack, sem = refs[:3], refs[3], refs[4]
        core, odd, half = place_ref[0], place_ref[1], place_ref[3] % 2
        copies = [
            pltpu.make_async_copy(psi_ref.at[sector, core, pl.ds(start * rows, rows)], part, sem.at[n])
            for n, (part, sector, start) in enumerate(zip(parts, (odd, 1 - odd, 1 - odd), (half, 0, 1), strict=True))
        ]
        copies.append(pltpu.make_async_copy(left_ref.at[0], pack.at[pl.ds(0, 2)], sem.at[3]))
        copies.append(pltpu.make_async_copy(right_ref.at[0], pack.at[pl.ds(2, 2)], sem.at[4]))
        for copy in copies:
            copy.start()
        for copy in copies:
            copy.wait()

    out = [pltpu.VMEM((rows, size), psi.dtype)] * 3 + [pltpu.VMEM((4, size, size), psi.dtype)]
    *parts, pack = call(
        body,
        "cut",
        out_shape=out,
        in_specs=[SMEM_SPEC] + [ANY_SPEC] * 3,
        out_specs=[VMEM_SPEC] * len(out),
        scratch_shapes=[pltpu.SemaphoreType.DMA((5,))],
    )(place, in_hbm(psi), in_hbm(left), in_hbm(right))
    return parts, pack


def copy_after(part, *after):
    def body(part_ref, *refs):
        out, sem = refs[-2:]
        copy = pltpu.make_async_copy(part_ref, out, sem)
        copy.start()
        copy.wait()

    return call(
        body,
        "copy_after",
        out_shape=pltpu.VMEM(part.shape, part.dtype),
        in_specs=[VMEM_SPEC] + [ANY_SPEC] * len(after),
        out_specs=VMEM_SPEC,
        scratch_shapes=[pltpu.SemaphoreType.DMA],
    )(in_vmem(part), *after)


def piece(step, secs, chips, scalars, halo, swapped, pack1, psi, left0, right0):
    size = psi.shape[-1]
    slots, height, count = len(halo), size // chips, chips // 2
    rows = size // 2
    near = [part for block in halo for part in block] + [pack1]
    far = [psi, left0, right0]

    def body(place, shift0, live0, other, *refs):
        halves, pack, refs = refs[: 2 * slots], refs[2 * slots], refs[2 * slots + 1 :]
        psi_ref, left_ref, right_ref, stay, first, final, own, left, right, inner, sem = refs
        core, odd, i, z = place[0], place[1], place[2], place[3]
        sector = step * odd + (1 - step) * (1 - odd)
        slot_of, weight_of = [], []
        for shift, live in zip((shift0[0], other[0]), (live0[0], other[1])):
            rel = sector - shift
            at = step - (2 * odd - 1) * shift
            if step == 0:
                slot = jnp.where(at == 2, 2, at + 2)
            else:
                slot = jnp.where(at >= 2, at - 1, at + 1)
            slot_of.append(jnp.where((rel == 0) | (rel == 1), slots + rel, slot))
            there = ((rel >= 0) | (i > 0)) & ((rel <= 1) | (i < secs - 1))
            weight_of.append(jnp.where(there, live, 0).astype(jnp.float32))

        def own_copy(term, index):
            return pltpu.make_async_copy(psi_ref.at[index, core], own.at[term], sem.at[term])

        for term in (1, 0):
            @pl.when(slot_of[term] >= slots)
            def _(term=term):
                own_copy(term, slot_of[term] - slots).start()
        left_copy = pltpu.make_async_copy(left_ref.at[0, sector], left, sem.at[2])
        right_copy = pltpu.make_async_copy(right_ref.at[0, sector], right, sem.at[3])
        left_copy.start()
        right_copy.start()

        order = [*range(1, chips, 2), *range(0, chips, 2)]
        for term in (1, 0):
            if term == 0:
                left_copy.wait()

            def left_rows(group, column, term=term):
                def at(r, k):
                    block = pl.ds(pl.multiple_of((z ^ r) * height + (core ^ k) * (height // 2), height // 2), height // 2)
                    columns = pl.ds(pl.multiple_of(column * rows, 128), rows)
                    return left[block, columns] if term == 0 else pack[sector, block, columns]

                return jnp.concatenate([at(r, k) for r in order[group * count : (group + 1) * count] for k in range(2)])

            def first_product(sources, columns, term=term, left_rows=left_rows):
                for group in range(2):
                    product = sum(
                        jnp.dot(left_rows(group, column), source(), preferred_element_type=jnp.float32)
                        for source, column in zip(sources, columns)
                    )
                    inner[term, pl.ds(group * rows, rows)] = product.astype(jnp.bfloat16)

            for k in range(slots):
                @pl.when(slot_of[term] == k)
                def _(k=k):
                    parity = z % 2 if swapped[k] else 0
                    sources = [lambda n=n: halves[2 * k + n][...] for n in range(2)]
                    first_product(sources, [parity, 1 - parity])

            @pl.when(slot_of[term] >= slots)
            def _(term=term):
                own_copy(term, 0).wait()
                first_product([lambda n=n: own[term, pl.ds(n * rows, rows)] for n in range(2)], [0, 1])

        right_copy.wait()
        for group in range(2):
            total = sum(
                lax.dot_general(
                    inner[term, pl.ds(group * rows, rows)],
                    right[...] if term == 0 else pack[2 + sector],
                    (((1,), (1,)), ((), ())),
                    preferred_element_type=jnp.float32,
                )
                * weight_of[term]
                for term in (1, 0)
            )
            for n in range(count):
                block = total[n * height : (n + 1) * height]
                if group == 1:
                    stay[n] = block
                elif n == 0:
                    final[...] = block.astype(final.dtype)
                else:
                    first[n - 1] = block.astype(first.dtype)

    return call(
        body,
        "piece",
        out_shape=(
            pltpu.VMEM((count, height, size), jnp.float32),
            pltpu.VMEM((count - 1, height, size), jnp.bfloat16),
            pltpu.VMEM((height, size), jnp.bfloat16),
        ),
        in_specs=[SMEM_SPEC] * 4 + [VMEM_SPEC] * len(near) + [ANY_SPEC] * len(far),
        out_specs=(VMEM_SPEC,) * 3,
        scratch_shapes=[
            pltpu.VMEM((2, size, size), jnp.bfloat16),
            pltpu.VMEM((size, size), jnp.bfloat16),
            pltpu.VMEM((size, size), jnp.bfloat16),
            pltpu.VMEM((2, size, size), jnp.bfloat16),
            pltpu.SemaphoreType.DMA((4,)),
        ],
    )(*scalars, *[in_vmem(x) for x in near], *[in_hbm(x) for x in far])


def sum_over_chips(stay, first, final, terms):
    pairs = [(d, d ^ 2) for d in range(terms)]
    got = lax.ppermute(first, "term", pairs)
    last = lax.ppermute(final, "term", pairs)
    mid = stay[1:] + got.astype(jnp.float32)
    keep = stay[0] + last.astype(jnp.float32)
    step = 4
    while step < terms:
        pairs = [(d, d ^ step) for d in range(terms)]
        last = lax.ppermute(mid[0].astype(jnp.bfloat16), "term", pairs)
        keep = keep + last.astype(jnp.float32)
        if mid.shape[0] > 1:
            got = lax.ppermute(mid[2::2].astype(jnp.bfloat16), "term", pairs)
            mid = mid[1::2] + got.astype(jnp.float32)
        step *= 2
    return keep


def local(psi, left_ops, right_ops, shift, live):
    secs, terms = lax.axis_size("sec"), lax.axis_size("term")
    size = psi.shape[-1]
    i, term = lax.axis_index("sec"), lax.axis_index("term")
    core, odd, z = term % 2, i % 2, term // 2
    cores = [(d, d ^ 1) for d in range(terms)]
    pairs = [(d, d ^ 1) for d in range(secs)]

    place = jnp.stack([core, odd, i, z]).astype(jnp.int32)
    parts, pack0 = cut(place, psi, left_ops, right_ops)
    near = [lax.ppermute(part, "sec", pairs) for part in parts]
    pack1 = lax.ppermute(pack0, "term", cores)
    other = lax.ppermute(jnp.concatenate([shift, live]), "term", cores)
    if secs == 4:
        turn = [(d, d ^ 2) for d in range(secs)]
        far = [lax.ppermute(part, "sec", turn) for part in near[:2]]
        far.append(lax.ppermute(copy_after(near[2], far[0]), "sec", turn))
    else:
        nexts = [(d, d + 1) for d in range(1, secs - 1, 2)]
        nexts = nexts + [(b, a) for a, b in nexts]
        far = [lax.ppermute(part, "sec", nexts) for part in parts]
    planes = [(d, d ^ 2) for d in range(terms)]
    near_first, near_second = (near[0], lax.ppermute(near[0], "term", planes)), near[1:]
    far_first, far_second = (far[0], lax.ppermute(far[0], "term", planes)), far[1:]

    scalars = (place, shift, live, other)
    outs = []
    for step in range(2):
        halo = (near_first, near_second, far_first) if step == 0 else (near_second, far_first, far_second)
        swapped = (True, False, True) if step == 0 else (False, True, False)
        blocks = piece(step, secs, terms // 2, scalars, halo, swapped, pack1, psi, left_ops, right_ops)
        total = sum_over_chips(*blocks, terms).astype(jnp.bfloat16)
        mine, others = total[: size // terms], total[size // terms :]
        got = lax.ppermute(others, "term", cores)
        outs.append(jnp.where(core == 0, jnp.stack([mine, got]), jnp.stack([got, mine])))
    return jnp.where(odd == 1, jnp.stack(outs), jnp.stack(outs[::-1]))


def solution(mesh):
    in_specs = (
        P("sec", None, None, None),
        P("term", "sec", None, None),
        P("term", "sec", None, None),
        P("term"),
        P("term"),
    )
    out_specs = P("sec", None, "term", None)
    return jax.shard_map(local, mesh=mesh, in_specs=in_specs, out_specs=out_specs, check_vma=False)
```

```python
import jax
import jax.numpy as jnp
from jax import lax
from jax.experimental import pallas as pl
from jax.experimental.pallas import tpu as pltpu
from jax.sharding import PartitionSpec as P

DQ = 2
VMEM_LIMIT = 12 * 1024 * 1024
SMEM_SPEC = pl.BlockSpec(memory_space=pltpu.SMEM)
VMEM_SPEC = pl.BlockSpec(memory_space=pltpu.VMEM)
ANY_SPEC = pl.BlockSpec(memory_space=pl.ANY)


def in_vmem(array):
    return pltpu.with_memory_space_constraint(array, pltpu.VMEM)


def in_hbm(array):
    return pltpu.with_memory_space_constraint(array, pltpu.HBM)


def call(body, name, **kwargs):
    return pl.pallas_call(
        body,
        compiler_params=pltpu.CompilerParams(vmem_limit_bytes=VMEM_LIMIT),
        cost_estimate=pl.CostEstimate(flops=1000, bytes_accessed=1000, transcendentals=0),
        name=name,
        **kwargs,
    )


def cut(place, psi, left, right):
    size = psi.shape[-1]
    rows = size // 2

    def body(place_ref, psi_ref, left_ref, right_ref, *refs):
        parts, pack, sem = refs[:3], refs[3], refs[4]
        core, odd, half = place_ref[0], place_ref[1], place_ref[3] % 2
        copies = [
            pltpu.make_async_copy(psi_ref.at[sector, core, pl.ds(start * rows, rows)], part, sem.at[n])
            for n, (part, sector, start) in enumerate(zip(parts, (odd, 1 - odd, 1 - odd), (half, 0, 1), strict=True))
        ]
        for k, ref in enumerate((left_ref, right_ref)):
            for s in range(2):
                at = pl.ds((2 * k + s) * size, size)
                copies.append(pltpu.make_async_copy(ref.at[0, s], pack.at[at], sem.at[3 + 2 * k + s]))
        for copy in copies:
            copy.start()
        number = lax.broadcasted_iota(jnp.int32, (16, size), 0)
        flags = jnp.where(number < 8, place_ref[4], place_ref[5])
        pack[pl.ds(4 * size, 16)] = flags.astype(jnp.float32).astype(pack.dtype)
        for copy in copies:
            copy.wait()

    out = [pltpu.VMEM((rows, size), psi.dtype)] * 3 + [pltpu.VMEM((4 * size + 16, size), psi.dtype)]
    *parts, pack = call(
        body,
        "cut",
        out_shape=out,
        in_specs=[SMEM_SPEC] + [ANY_SPEC] * 3,
        out_specs=[VMEM_SPEC] * 4,
        scratch_shapes=[pltpu.SemaphoreType.DMA((7,))],
    )(place, in_hbm(psi), in_hbm(left), in_hbm(right))
    return parts, pack


def copy_after(part, *after):
    def body(part_ref, *refs):
        out, sem = refs[-2:]
        copy = pltpu.make_async_copy(part_ref, out, sem)
        copy.start()
        copy.wait()

    return call(
        body,
        "copy_after",
        out_shape=pltpu.VMEM(part.shape, part.dtype),
        in_specs=[VMEM_SPEC] + [ANY_SPEC] * len(after),
        out_specs=VMEM_SPEC,
        scratch_shapes=[pltpu.SemaphoreType.DMA],
    )(in_vmem(part), *after)


def piece(step, secs, chips, bits, scalars, halo, swapped, pack1, psi, left0, right0):
    def relative(q):
        return sum((q >> k & 1) << bit for k, bit in enumerate(bits))

    size = psi.shape[-1]
    parked = step == 0
    slots, height, count = len(halo), size // chips, chips // 2
    rows = size // 2
    near = [part for block in halo for part in block] + [pack1]
    far = [psi, left0, right0]

    def body(place, *refs):
        halves, pack, refs = refs[: 2 * slots], refs[2 * slots], refs[2 * slots + 1 :]
        psi_ref, left_ref, right_ref, stay, gone, own, left, right, inner, kept, sem = refs
        core, odd, i, z = place[0], place[1], place[2], place[3]
        sector = step * odd + (1 - step) * (1 - odd)
        flags = pack[pl.ds(4 * size, 16), pl.ds(0, 128)].astype(jnp.float32)
        shift1, live1 = (jnp.max(part).astype(jnp.int32) for part in (flags[:8], flags[8:]))
        slot_of, weight_of = [], []
        for shift, live in ((place[4], place[5]), (shift1, live1)):
            rel = sector - shift
            at = step - (2 * odd - 1) * shift
            if step == 0:
                slot = jnp.where(at == 2, 2, at + 2)
            else:
                slot = jnp.where(at >= 2, at - 1, at + 1)
            slot_of.append(jnp.where((rel == 0) | (rel == 1), slots + rel, slot))
            there = ((rel >= 0) | (i > 0)) & ((rel <= 1) | (i < secs - 1))
            weight_of.append(jnp.where(there, live, 0).astype(jnp.float32))

        def own_copy(term, index):
            return pltpu.make_async_copy(psi_ref.at[index, core], own.at[term], sem.at[term])

        for term in (1, 0):
            @pl.when(slot_of[term] >= slots)
            def _(term=term):
                own_copy(term, slot_of[term] - slots).start()
        left_copy = pltpu.make_async_copy(left_ref.at[0, sector], left, sem.at[2])
        right_copy = pltpu.make_async_copy(right_ref.at[0, sector], right, sem.at[3])
        left_copy.start()
        right_copy.start()

        order = [relative(q) for q in [*range(1, chips, 2), *range(0, chips, 2)]]
        for term in (1, 0):
            if term == 0:
                left_copy.wait()

            def left_rows(group, column, term=term):
                def at(r, k):
                    start = (z ^ r) * height + (core ^ k) * (height // 2)
                    start = start if term == 0 else start + sector * size
                    block = pl.ds(pl.multiple_of(start, height // 2), height // 2)
                    columns = pl.ds(pl.multiple_of(column * rows, 128), rows)
                    return left[block, columns] if term == 0 else pack[block, columns]

                return jnp.concatenate([at(r, k) for r in order[group * count : (group + 1) * count] for k in range(2)])

            def first_product(sources, columns, term=term, left_rows=left_rows):
                for group in range(2):
                    product = sum(
                        jnp.dot(left_rows(group, column), source(), preferred_element_type=jnp.float32)
                        for source, column in zip(sources, columns)
                    )
                    inner[term, pl.ds(group * rows, rows)] = product.astype(jnp.bfloat16)

            for k in range(slots):
                @pl.when(slot_of[term] == k)
                def _(k=k):
                    parity = z % 2 if swapped[k] else 0
                    sources = [lambda n=n: halves[2 * k + n][...] for n in range(2)]
                    first_product(sources, [parity, 1 - parity])

            @pl.when(slot_of[term] >= slots)
            def _(term=term):
                own_copy(term, 0).wait()
                first_product([lambda n=n: own[term, pl.ds(n * rows, rows)] for n in range(2)], [0, 1])

        right_copy.wait()
        stay_copy = pltpu.make_async_copy(kept, stay, sem.at[4]) if parked else None
        for group in (1, 0):
            total = sum(
                lax.dot_general(
                    inner[term, pl.ds(group * rows, rows)],
                    right[...] if term == 0 else pack[pl.ds(pl.multiple_of((2 + sector) * size, size), size)],
                    (((1,), (1,)), ((), ())),
                    preferred_element_type=jnp.float32,
                )
                * weight_of[term]
                for term in (1, 0)
            )
            for n in range(count):
                block = total[n * height : (n + 1) * height]
                if group == 0:
                    gone[n] = block.astype(gone.dtype)
                else:
                    (kept if parked else stay)[n] = block
            if group == 1 and parked:
                stay_copy.start()
        if parked:
            stay_copy.wait()

    stay_shape = (count, height, size)
    outs = [pltpu.HBM(stay_shape, jnp.float32) if parked else pltpu.VMEM(stay_shape, jnp.float32)]
    outs.append(pltpu.VMEM(stay_shape, jnp.bfloat16))
    return call(
        body,
        "piece",
        out_shape=outs,
        in_specs=[SMEM_SPEC] + [VMEM_SPEC] * len(near) + [ANY_SPEC] * len(far),
        out_specs=[ANY_SPEC if parked else VMEM_SPEC] + [VMEM_SPEC] * (len(outs) - 1),
        scratch_shapes=[
            pltpu.VMEM((2, size, size), jnp.bfloat16),
            pltpu.VMEM((size, size), jnp.bfloat16),
            pltpu.VMEM((size, size), jnp.bfloat16),
            pltpu.VMEM((2, size, size), jnp.bfloat16),
            pltpu.VMEM((count, height, size), jnp.float32),
            pltpu.SemaphoreType.DMA((5,)),
        ],
    )(*scalars, *[in_vmem(x) for x in near], *[in_hbm(x) for x in far])


def sum_over_chips(stay, gone, bits, terms):
    for bit in bits:
        pairs = [(d, d ^ (2 << bit)) for d in range(terms)]
        total = stay + lax.ppermute(gone, "term", pairs).astype(jnp.float32)
        stay, gone = total[::2], total[1::2].astype(jnp.bfloat16)
    return stay[0]


def local(psi, left_ops, right_ops, shift, live):
    secs, terms = lax.axis_size("sec"), lax.axis_size("term")
    size = psi.shape[-1]
    i, term = lax.axis_index("sec"), lax.axis_index("term")
    core, odd, z = term % 2, i % 2, term // 2
    cores = [(d, d ^ 1) for d in range(terms)]
    pairs = [(d, d ^ 1) for d in range(secs)]

    place = jnp.stack([core, odd, i, z, shift[0], live[0]]).astype(jnp.int32)
    parts, pack0 = cut(place, psi, left_ops, right_ops)
    near = [lax.ppermute(part, "sec", pairs) for part in parts]
    pack1 = lax.ppermute(pack0, "term", cores)
    if secs == 4:
        turn = [(d, d ^ 2) for d in range(secs)]
        far = [lax.ppermute(part, "sec", turn) for part in near[:2]]
        far.append(lax.ppermute(copy_after(near[2], far[0]), "sec", turn))
    else:
        nexts = [(d, d + 1) for d in range(1, secs - 1, 2)]
        nexts = nexts + [(b, a) for a, b in nexts]
        far = [lax.ppermute(part, "sec", nexts) for part in parts]
    planes = [(d, d ^ 2) for d in range(terms)]
    near_first, near_second = (near[0], lax.ppermute(near[0], "term", planes)), near[1:]
    far_first, far_second = (far[0], lax.ppermute(copy_after(far[0], near[1]), "term", planes)), far[1:]

    scalars = (place,)
    outs = []
    for step in range(2):
        halo = (near_first, near_second, far_first) if step == 0 else (near_second, far_first, far_second)
        swapped = (True, False, True) if step == 0 else (False, True, False)
        bits = list(range((terms // 2).bit_length() - 1))
        blocks = piece(step, secs, terms // 2, bits, scalars, halo, swapped, pack1, psi, left_ops, right_ops)
        total = sum_over_chips(*blocks, bits, terms).astype(jnp.bfloat16)
        mine, others = total[: size // terms], total[size // terms :]
        got = lax.ppermute(others, "term", cores)
        outs.append(jnp.where(core == 0, jnp.stack([mine, got]), jnp.stack([got, mine])))
    return jnp.where(odd == 1, jnp.stack(outs), jnp.stack(outs[::-1]))


def solution(mesh):
    in_specs = (
        P("sec", None, None, None),
        P("term", "sec", None, None),
        P("term", "sec", None, None),
        P("term"),
        P("term"),
    )
    out_specs = P("sec", None, "term", None)
    return jax.shard_map(local, mesh=mesh, in_specs=in_specs, out_specs=out_specs, check_vma=False)
```

```python
import jax
import jax.numpy as jnp
from jax import lax
from jax.experimental import pallas as pl
from jax.experimental.pallas import tpu as pltpu
from jax.sharding import PartitionSpec as P

DQ = 2
VMEM_LIMIT = 12 * 1024 * 1024
SMEM_SPEC = pl.BlockSpec(memory_space=pltpu.SMEM)
VMEM_SPEC = pl.BlockSpec(memory_space=pltpu.VMEM)
ANY_SPEC = pl.BlockSpec(memory_space=pl.ANY)


def in_vmem(array):
    return pltpu.with_memory_space_constraint(array, pltpu.VMEM)


def in_hbm(array):
    return pltpu.with_memory_space_constraint(array, pltpu.HBM)


def call(body, name, **kwargs):
    return pl.pallas_call(
        body,
        compiler_params=pltpu.CompilerParams(vmem_limit_bytes=VMEM_LIMIT),
        cost_estimate=pl.CostEstimate(flops=1000, bytes_accessed=1000, transcendentals=0),
        name=name,
        **kwargs,
    )


def cut(place, psi, left, right):
    size = psi.shape[-1]
    rows = size // 2

    def body(place_ref, psi_ref, left_ref, right_ref, *refs):
        parts, pack, sem = refs[:3], refs[3], refs[4]
        core, odd, half = place_ref[0], place_ref[1], place_ref[3] % 2
        copies = [
            pltpu.make_async_copy(psi_ref.at[sector, core, pl.ds(start * rows, rows)], part, sem.at[n])
            for n, (part, sector, start) in enumerate(zip(parts, (odd, 1 - odd, 1 - odd), (half, 0, 1), strict=True))
        ]
        for k, ref in enumerate((left_ref, right_ref)):
            for s in range(2):
                at = pl.ds((2 * k + s) * size, size)
                copies.append(pltpu.make_async_copy(ref.at[0, s], pack.at[at], sem.at[3 + 2 * k + s]))
        for copy in copies:
            copy.start()
        number = lax.broadcasted_iota(jnp.int32, (16, size), 0)
        flags = jnp.where(number < 8, place_ref[4], place_ref[5])
        pack[pl.ds(4 * size, 16)] = flags.astype(jnp.float32).astype(pack.dtype)
        for copy in copies:
            copy.wait()

    out = [pltpu.VMEM((rows, size), psi.dtype)] * 3 + [pltpu.VMEM((4 * size + 16, size), psi.dtype)]
    *parts, pack = call(
        body,
        "cut",
        out_shape=out,
        in_specs=[SMEM_SPEC] + [ANY_SPEC] * 3,
        out_specs=[VMEM_SPEC] * 4,
        scratch_shapes=[pltpu.SemaphoreType.DMA((7,))],
    )(place, in_hbm(psi), in_hbm(left), in_hbm(right))
    return parts, pack


def copy_after(part, *after):
    def body(part_ref, *refs):
        out, sem = refs[-2:]
        copy = pltpu.make_async_copy(part_ref, out, sem)
        copy.start()
        copy.wait()

    return call(
        body,
        "copy_after",
        out_shape=pltpu.VMEM(part.shape, part.dtype),
        in_specs=[VMEM_SPEC] + [ANY_SPEC] * len(after),
        out_specs=VMEM_SPEC,
        scratch_shapes=[pltpu.SemaphoreType.DMA],
    )(in_vmem(part), *after)


def piece(step, secs, chips, bits, scalars, halo, swapped, pack1, psi, left0, right0):
    def relative(q):
        return sum((q >> k & 1) << bit for k, bit in enumerate(bits))

    size = psi.shape[-1]
    parked = step == 0
    slots, height, count = len(halo), size // chips, chips // 2
    rows = size // 2
    near = [part for block in halo for part in block] + [pack1]
    far = [psi, left0, right0]

    def body(place, *refs):
        halves, pack, refs = refs[: 2 * slots], refs[2 * slots], refs[2 * slots + 1 :]
        psi_ref, left_ref, right_ref, stay, gone, own, left, right, inner, kept, sem = refs
        core, odd, i, z = place[0], place[1], place[2], place[3]
        sector = step * odd + (1 - step) * (1 - odd)
        flags = pack[pl.ds(4 * size, 16), pl.ds(0, 128)].astype(jnp.float32)
        shift1, live1 = (jnp.max(part).astype(jnp.int32) for part in (flags[:8], flags[8:]))
        slot_of, weight_of = [], []
        for shift, live in ((place[4], place[5]), (shift1, live1)):
            rel = sector - shift
            at = step - (2 * odd - 1) * shift
            if step == 0:
                slot = jnp.where(at == 2, 2, at + 2)
            else:
                slot = jnp.where(at >= 2, at - 1, at + 1)
            slot_of.append(jnp.where((rel == 0) | (rel == 1), slots + rel, slot))
            there = ((rel >= 0) | (i > 0)) & ((rel <= 1) | (i < secs - 1))
            weight_of.append(jnp.where(there, live, 0).astype(jnp.float32))

        def own_copy(term, index):
            return pltpu.make_async_copy(psi_ref.at[index, core], own.at[term], sem.at[term])

        for term in (1, 0):
            @pl.when(slot_of[term] >= slots)
            def _(term=term):
                own_copy(term, slot_of[term] - slots).start()
        left_copy = pltpu.make_async_copy(left_ref.at[0, sector], left, sem.at[2])
        right_copy = pltpu.make_async_copy(right_ref.at[0, sector], right, sem.at[3])
        left_copy.start()
        right_copy.start()

        order = [relative(q) for q in [*range(1, chips, 2), *range(0, chips, 2)]]
        for term in (1, 0):
            if term == 0:
                left_copy.wait()

            def left_rows(group, column, term=term):
                def at(r, k):
                    start = (z ^ r) * height + (core ^ k) * (height // 2)
                    start = start if term == 0 else start + sector * size
                    block = pl.ds(pl.multiple_of(start, height // 2), height // 2)
                    columns = pl.ds(pl.multiple_of(column * rows, 128), rows)
                    return left[block, columns] if term == 0 else pack[block, columns]

                return jnp.concatenate([at(r, k) for r in order[group * count : (group + 1) * count] for k in range(2)])

            def first_product(sources, columns, term=term, left_rows=left_rows):
                for group in range(2):
                    product = sum(
                        jnp.dot(left_rows(group, column), source(), preferred_element_type=jnp.float32)
                        for source, column in zip(sources, columns)
                    )
                    inner[term, pl.ds(group * rows, rows)] = product.astype(jnp.bfloat16)

            for k in range(slots):
                @pl.when(slot_of[term] == k)
                def _(k=k):
                    parity = z % 2 if swapped[k] else 0
                    sources = [lambda n=n: halves[2 * k + n][...] for n in range(2)]
                    first_product(sources, [parity, 1 - parity])

            @pl.when(slot_of[term] >= slots)
            def _(term=term):
                own_copy(term, 0).wait()
                first_product([lambda n=n: own[term, pl.ds(n * rows, rows)] for n in range(2)], [0, 1])

        right_copy.wait()
        stay_copy = pltpu.make_async_copy(kept, stay, sem.at[4]) if parked else None
        for group in (1, 0):
            total = sum(
                lax.dot_general(
                    inner[term, pl.ds(group * rows, rows)],
                    right[...] if term == 0 else pack[pl.ds(pl.multiple_of((2 + sector) * size, size), size)],
                    (((1,), (1,)), ((), ())),
                    preferred_element_type=jnp.float32,
                )
                * weight_of[term]
                for term in (1, 0)
            )
            for n in range(count):
                block = total[n * height : (n + 1) * height]
                if group == 0:
                    gone[n] = block.astype(gone.dtype)
                else:
                    (kept if parked else stay)[n] = block
            if group == 1 and parked:
                stay_copy.start()
        if parked:
            stay_copy.wait()

    stay_shape = (count, height, size)
    outs = [pltpu.HBM(stay_shape, jnp.float32) if parked else pltpu.VMEM(stay_shape, jnp.float32)]
    outs.append(pltpu.VMEM(stay_shape, jnp.bfloat16))
    return call(
        body,
        "piece",
        out_shape=outs,
        in_specs=[SMEM_SPEC] + [VMEM_SPEC] * len(near) + [ANY_SPEC] * len(far),
        out_specs=[ANY_SPEC if parked else VMEM_SPEC] + [VMEM_SPEC] * (len(outs) - 1),
        scratch_shapes=[
            pltpu.VMEM((2, size, size), jnp.bfloat16),
            pltpu.VMEM((size, size), jnp.bfloat16),
            pltpu.VMEM((size, size), jnp.bfloat16),
            pltpu.VMEM((2, size, size), jnp.bfloat16),
            pltpu.VMEM((count, height, size), jnp.float32),
            pltpu.SemaphoreType.DMA((5,)),
        ],
    )(*scalars, *[in_vmem(x) for x in near], *[in_hbm(x) for x in far])


def sum_over_chips(stay, gone, bits, terms, direct):
    half = stay.shape[1] // 2
    cores = [(d, d ^ 1) for d in range(terms)]
    for n, bit in enumerate(bits):
        pairs = [(d, d ^ (2 << bit)) for d in range(terms)]
        if direct and n == len(bits) - 1:
            across = [(d, d ^ (2 << bit) ^ 1) for d in range(terms)]
            swapped = lax.ppermute(stay[0], "term", cores)[half:]
            mine = stay[0, :half] + lax.ppermute(gone[0, :half], "term", pairs).astype(jnp.float32)
            others = swapped + lax.ppermute(gone[0, half:], "term", across).astype(jnp.float32)
            return mine.astype(jnp.bfloat16), others.astype(jnp.bfloat16)
        total = stay + lax.ppermute(gone, "term", pairs).astype(jnp.float32)
        stay, gone = total[::2], total[1::2].astype(jnp.bfloat16)
    total = stay[0].astype(jnp.bfloat16)
    return total[:half], lax.ppermute(total[half:], "term", cores)


def local(psi, left_ops, right_ops, shift, live):
    secs, terms = lax.axis_size("sec"), lax.axis_size("term")
    size = psi.shape[-1]
    i, term = lax.axis_index("sec"), lax.axis_index("term")
    core, odd, z = term % 2, i % 2, term // 2
    cores = [(d, d ^ 1) for d in range(terms)]
    pairs = [(d, d ^ 1) for d in range(secs)]

    place = jnp.stack([core, odd, i, z, shift[0], live[0]]).astype(jnp.int32)
    parts, pack0 = cut(place, psi, left_ops, right_ops)
    near = [lax.ppermute(part, "sec", pairs) for part in parts]
    pack1 = lax.ppermute(pack0, "term", cores)
    if secs == 4:
        turn = [(d, d ^ 2) for d in range(secs)]
        far = [lax.ppermute(part, "sec", turn) for part in near[:2]]
        far.append(lax.ppermute(copy_after(near[2], far[0]), "sec", turn))
    else:
        nexts = [(d, d + 1) for d in range(1, secs - 1, 2)]
        nexts = nexts + [(b, a) for a, b in nexts]
        far = [lax.ppermute(part, "sec", nexts) for part in parts]
    planes = [(d, d ^ 2) for d in range(terms)]
    near_first, near_second = (near[0], lax.ppermute(near[0], "term", planes)), near[1:]
    far_first, far_second = (far[0], lax.ppermute(copy_after(far[0], near[1], near_first[1]), "term", planes)), far[1:]

    scalars = (place,)
    outs = []
    for step in range(2):
        halo = (near_first, near_second, far_first) if step == 0 else (near_second, far_first, far_second)
        swapped = (True, False, True) if step == 0 else (False, True, False)
        bits = list(range((terms // 2).bit_length() - 1))
        blocks = piece(step, secs, terms // 2, bits, scalars, halo, swapped, pack1, psi, left_ops, right_ops)
        mine, got = sum_over_chips(*blocks, bits, terms, step == 1)
        outs.append(jnp.where(core == 0, jnp.stack([mine, got]), jnp.stack([got, mine])))
    return jnp.where(odd == 1, jnp.stack(outs), jnp.stack(outs[::-1]))


def solution(mesh):
    in_specs = (
        P("sec", None, None, None),
        P("term", "sec", None, None),
        P("term", "sec", None, None),
        P("term"),
        P("term"),
    )
    out_specs = P("sec", None, "term", None)
    return jax.shard_map(local, mesh=mesh, in_specs=in_specs, out_specs=out_specs, check_vma=False)
```

```python
import jax
import jax.numpy as jnp
from jax import lax
from jax.experimental import pallas as pl
from jax.experimental.pallas import tpu as pltpu
from jax.sharding import PartitionSpec as P

DQ = 2
VMEM_LIMIT = 12 * 1024 * 1024
SMEM_SPEC = pl.BlockSpec(memory_space=pltpu.SMEM)
VMEM_SPEC = pl.BlockSpec(memory_space=pltpu.VMEM)
ANY_SPEC = pl.BlockSpec(memory_space=pl.ANY)


def in_vmem(array):
    return pltpu.with_memory_space_constraint(array, pltpu.VMEM)


def in_hbm(array):
    return pltpu.with_memory_space_constraint(array, pltpu.HBM)


def call(body, name, **kwargs):
    return pl.pallas_call(
        body,
        compiler_params=pltpu.CompilerParams(vmem_limit_bytes=VMEM_LIMIT),
        cost_estimate=pl.CostEstimate(flops=1000, bytes_accessed=1000, transcendentals=0),
        name=name,
        **kwargs,
    )


def cut(place, psi, left, right):
    size = psi.shape[-1]
    rows = size // 2

    def body(place_ref, psi_ref, left_ref, right_ref, *refs):
        parts, pack, sem = refs[:3], refs[3], refs[4]
        core, odd, half = place_ref[0], place_ref[1], place_ref[3] % 2
        copies = [
            pltpu.make_async_copy(psi_ref.at[sector, core, pl.ds(start * rows, rows)], part, sem.at[n])
            for n, (part, sector, start) in enumerate(zip(parts, (odd, 1 - odd, 1 - odd), (half, 0, 1), strict=True))
        ]
        for k, ref in enumerate((left_ref, right_ref)):
            for s in range(2):
                at = pl.ds((2 * k + s) * size, size)
                copies.append(pltpu.make_async_copy(ref.at[0, s], pack.at[at], sem.at[3 + 2 * k + s]))
        for copy in copies:
            copy.start()
        number = lax.broadcasted_iota(jnp.int32, (16, size), 0)
        flags = jnp.where(number < 8, place_ref[4], place_ref[5])
        pack[pl.ds(4 * size, 16)] = flags.astype(jnp.float32).astype(pack.dtype)
        for copy in copies:
            copy.wait()

    out = [pltpu.VMEM((rows, size), psi.dtype)] * 3 + [pltpu.VMEM((4 * size + 16, size), psi.dtype)]
    *parts, pack = call(
        body,
        "cut",
        out_shape=out,
        in_specs=[SMEM_SPEC] + [ANY_SPEC] * 3,
        out_specs=[VMEM_SPEC] * 4,
        scratch_shapes=[pltpu.SemaphoreType.DMA((7,))],
    )(place, in_hbm(psi), in_hbm(left), in_hbm(right))
    return parts, pack


def copy_after(part, *after):
    def body(part_ref, *refs):
        out, sem = refs[-2:]
        copy = pltpu.make_async_copy(part_ref, out, sem)
        copy.start()
        copy.wait()

    return call(
        body,
        "copy_after",
        out_shape=pltpu.VMEM(part.shape, part.dtype),
        in_specs=[VMEM_SPEC] + [ANY_SPEC] * len(after),
        out_specs=VMEM_SPEC,
        scratch_shapes=[pltpu.SemaphoreType.DMA],
    )(in_vmem(part), *after)


def piece(step, secs, chips, bits, scalars, halo, swapped, pack1, pack0, psi):
    def relative(q):
        return sum((q >> k & 1) << bit for k, bit in enumerate(bits))

    size = psi.shape[-1]
    parked = step == 0
    slots, height, count = len(halo), size // chips, chips // 2
    rows = size // 2
    near = [part for block in halo for part in block] + [pack1, pack0]
    far = [psi]

    def body(place, *refs):
        halves, pack, own_pack, refs = refs[: 2 * slots], refs[2 * slots], refs[2 * slots + 1], refs[2 * slots + 2 :]
        psi_ref, stay, gone, own, inner, kept, sem = refs
        core, odd, i, z = place[0], place[1], place[2], place[3]
        sector = step * odd + (1 - step) * (1 - odd)
        flags = pack[pl.ds(4 * size, 16), pl.ds(0, 128)].astype(jnp.float32)
        shift1, live1 = (jnp.max(part).astype(jnp.int32) for part in (flags[:8], flags[8:]))
        slot_of, weight_of = [], []
        for shift, live in ((place[4], place[5]), (shift1, live1)):
            rel = sector - shift
            at = step - (2 * odd - 1) * shift
            if step == 0:
                slot = jnp.where(at == 2, 2, at + 2)
            else:
                slot = jnp.where(at >= 2, at - 1, at + 1)
            slot_of.append(jnp.where((rel == 0) | (rel == 1), slots + rel, slot))
            there = ((rel >= 0) | (i > 0)) & ((rel <= 1) | (i < secs - 1))
            weight_of.append(jnp.where(there, live, 0).astype(jnp.float32))

        def own_copy(term, index):
            return pltpu.make_async_copy(psi_ref.at[index, core], own.at[term], sem.at[term])

        for term in (1, 0):
            @pl.when(slot_of[term] >= slots)
            def _(term=term):
                own_copy(term, slot_of[term] - slots).start()
        order = [relative(q) for q in [*range(1, chips, 2), *range(0, chips, 2)]]
        for term in (1, 0):
            def left_rows(group, column, term=term):
                def at(r, k):
                    start = (z ^ r) * height + (core ^ k) * (height // 2)
                    start = start + sector * size
                    block = pl.ds(pl.multiple_of(start, height // 2), height // 2)
                    columns = pl.ds(pl.multiple_of(column * rows, 128), rows)
                    return (own_pack, pack)[term][block, columns]

                return jnp.concatenate([at(r, k) for r in order[group * count : (group + 1) * count] for k in range(2)])

            def first_product(sources, columns, term=term, left_rows=left_rows):
                for group in range(2):
                    product = sum(
                        jnp.dot(left_rows(group, column), source(), preferred_element_type=jnp.float32)
                        for source, column in zip(sources, columns)
                    )
                    inner[term, pl.ds(group * rows, rows)] = product.astype(jnp.bfloat16)

            for k in range(slots):
                @pl.when(slot_of[term] == k)
                def _(k=k):
                    parity = z % 2 if swapped[k] else 0
                    sources = [lambda n=n: halves[2 * k + n][...] for n in range(2)]
                    first_product(sources, [parity, 1 - parity])

            @pl.when(slot_of[term] >= slots)
            def _(term=term):
                own_copy(term, 0).wait()
                first_product([lambda n=n: own[term, pl.ds(n * rows, rows)] for n in range(2)], [0, 1])

        stay_copy = pltpu.make_async_copy(kept, stay, sem.at[4]) if parked else None
        for group in (1, 0):
            total = sum(
                lax.dot_general(
                    inner[term, pl.ds(group * rows, rows)],
                    (own_pack, pack)[term][pl.ds(pl.multiple_of((2 + sector) * size, size), size)],
                    (((1,), (1,)), ((), ())),
                    preferred_element_type=jnp.float32,
                )
                * weight_of[term]
                for term in (1, 0)
            )
            for n in range(count):
                block = total[n * height : (n + 1) * height]
                if group == 0:
                    gone[n] = block.astype(gone.dtype)
                else:
                    (kept if parked else stay)[n] = block
            if group == 1 and parked:
                stay_copy.start()
        if parked:
            stay_copy.wait()

    stay_shape = (count, height, size)
    outs = [pltpu.HBM(stay_shape, jnp.float32) if parked else pltpu.VMEM(stay_shape, jnp.float32)]
    outs.append(pltpu.VMEM(stay_shape, jnp.bfloat16))
    return call(
        body,
        "piece",
        out_shape=outs,
        in_specs=[SMEM_SPEC] + [VMEM_SPEC] * len(near) + [ANY_SPEC] * len(far),
        out_specs=[ANY_SPEC if parked else VMEM_SPEC] + [VMEM_SPEC] * (len(outs) - 1),
        scratch_shapes=[
            pltpu.VMEM((2, size, size), jnp.bfloat16),
            pltpu.VMEM((2, size, size), jnp.bfloat16),
            pltpu.VMEM((count, height, size), jnp.float32),
            pltpu.SemaphoreType.DMA((5,)),
        ],
    )(*scalars, *[in_vmem(x) for x in near], *[in_hbm(x) for x in far])


def sum_over_chips(stay, gone, bits, terms, direct):
    half = stay.shape[1] // 2
    cores = [(d, d ^ 1) for d in range(terms)]
    for n, bit in enumerate(bits):
        pairs = [(d, d ^ (2 << bit)) for d in range(terms)]
        if direct and n == len(bits) - 1:
            across = [(d, d ^ (2 << bit) ^ 1) for d in range(terms)]
            swapped = lax.ppermute(stay[0], "term", cores)[half:]
            mine = stay[0, :half] + lax.ppermute(gone[0, :half], "term", pairs).astype(jnp.float32)
            others = swapped + lax.ppermute(gone[0, half:], "term", across).astype(jnp.float32)
            return mine.astype(jnp.bfloat16), others.astype(jnp.bfloat16)
        total = stay + lax.ppermute(gone, "term", pairs).astype(jnp.float32)
        stay, gone = total[::2], total[1::2].astype(jnp.bfloat16)
    total = stay[0].astype(jnp.bfloat16)
    return total[:half], lax.ppermute(total[half:], "term", cores)


def local(psi, left_ops, right_ops, shift, live):
    secs, terms = lax.axis_size("sec"), lax.axis_size("term")
    size = psi.shape[-1]
    i, term = lax.axis_index("sec"), lax.axis_index("term")
    core, odd, z = term % 2, i % 2, term // 2
    cores = [(d, d ^ 1) for d in range(terms)]
    pairs = [(d, d ^ 1) for d in range(secs)]

    place = jnp.stack([core, odd, i, z, shift[0], live[0]]).astype(jnp.int32)
    parts, pack0 = cut(place, psi, left_ops, right_ops)
    near = [lax.ppermute(part, "sec", pairs) for part in parts]
    pack1 = lax.ppermute(pack0, "term", cores)
    if secs == 4:
        turn = [(d, d ^ 2) for d in range(secs)]
        far = [lax.ppermute(part, "sec", turn) for part in near[:2]]
        far.append(lax.ppermute(copy_after(near[2], far[0]), "sec", turn))
    else:
        nexts = [(d, d + 1) for d in range(1, secs - 1, 2)]
        nexts = nexts + [(b, a) for a, b in nexts]
        far = [lax.ppermute(part, "sec", nexts) for part in parts]
    planes = [(d, d ^ 2) for d in range(terms)]
    near_first, near_second = (near[0], lax.ppermute(near[0], "term", planes)), near[1:]
    far_first, far_second = (far[0], lax.ppermute(copy_after(far[0], near[1], near_first[1]), "term", planes)), far[1:]

    scalars = (place,)
    outs = []
    for step in range(2):
        halo = (near_first, near_second, far_first) if step == 0 else (near_second, far_first, far_second)
        swapped = (True, False, True) if step == 0 else (False, True, False)
        bits = list(range((terms // 2).bit_length() - 1))
        blocks = piece(step, secs, terms // 2, bits, scalars, halo, swapped, pack1, pack0, psi)
        mine, got = sum_over_chips(*blocks, bits, terms, step == 1)
        outs.append(jnp.where(core == 0, jnp.stack([mine, got]), jnp.stack([got, mine])))
    return jnp.where(odd == 1, jnp.stack(outs), jnp.stack(outs[::-1]))


def solution(mesh):
    in_specs = (
        P("sec", None, None, None),
        P("term", "sec", None, None),
        P("term", "sec", None, None),
        P("term"),
        P("term"),
    )
    out_specs = P("sec", None, "term", None)
    return jax.shard_map(local, mesh=mesh, in_specs=in_specs, out_specs=out_specs, check_vma=False)
```

```python
import jax
import jax.numpy as jnp
from jax import lax
from jax.experimental import pallas as pl
from jax.experimental.pallas import tpu as pltpu
from jax.sharding import PartitionSpec as P

DQ = 2
VMEM_LIMIT = 12 * 1024 * 1024
SMEM_SPEC = pl.BlockSpec(memory_space=pltpu.SMEM)
VMEM_SPEC = pl.BlockSpec(memory_space=pltpu.VMEM)
ANY_SPEC = pl.BlockSpec(memory_space=pl.ANY)


def in_vmem(array):
    return pltpu.with_memory_space_constraint(array, pltpu.VMEM)


def in_hbm(array):
    return pltpu.with_memory_space_constraint(array, pltpu.HBM)


def call(body, name, **kwargs):
    return pl.pallas_call(
        body,
        compiler_params=pltpu.CompilerParams(vmem_limit_bytes=VMEM_LIMIT),
        cost_estimate=pl.CostEstimate(flops=1000, bytes_accessed=1000, transcendentals=0),
        name=name,
        **kwargs,
    )


def cut(place, psi, left, right):
    size = psi.shape[-1]
    rows = size // 2

    def body(place_ref, psi_ref, left_ref, right_ref, *refs):
        parts, pack, sem = refs[:4], refs[4], refs[5]
        core, odd, half = place_ref[0], place_ref[1], place_ref[3] % 2
        copies = [
            pltpu.make_async_copy(psi_ref.at[sector, core, pl.ds(start * rows, rows)], part, sem.at[n])
            for n, (part, sector, start) in enumerate(zip(parts, (odd, 1 - odd, 1 - odd, odd), (half, 0, 1, 1 - half), strict=True))
        ]
        for k, ref in enumerate((left_ref, right_ref)):
            for s in range(2):
                at = pl.ds((2 * k + s) * size, size)
                copies.append(pltpu.make_async_copy(ref.at[0, s], pack.at[at], sem.at[4 + 2 * k + s]))
        for copy in copies:
            copy.start()
        number = lax.broadcasted_iota(jnp.int32, (16, size), 0)
        flags = jnp.where(number < 8, place_ref[4], place_ref[5])
        pack[pl.ds(4 * size, 16)] = flags.astype(jnp.float32).astype(pack.dtype)
        for copy in copies:
            copy.wait()

    out = [pltpu.VMEM((rows, size), psi.dtype)] * 4 + [pltpu.VMEM((4 * size + 16, size), psi.dtype)]
    *parts, pack = call(
        body,
        "cut",
        out_shape=out,
        in_specs=[SMEM_SPEC] + [ANY_SPEC] * 3,
        out_specs=[VMEM_SPEC] * 5,
        scratch_shapes=[pltpu.SemaphoreType.DMA((8,))],
    )(place, in_hbm(psi), in_hbm(left), in_hbm(right))
    return parts, pack


def copy_after(part, *after):
    def body(part_ref, *refs):
        out, sem = refs[-2:]
        copy = pltpu.make_async_copy(part_ref, out, sem)
        copy.start()
        copy.wait()

    return call(
        body,
        "copy_after",
        out_shape=pltpu.VMEM(part.shape, part.dtype),
        in_specs=[VMEM_SPEC] + [ANY_SPEC] * len(after),
        out_specs=VMEM_SPEC,
        scratch_shapes=[pltpu.SemaphoreType.DMA],
    )(in_vmem(part), *after)


def piece(step, secs, chips, bits, scalars, sources, swapped, pack1, pack0):
    def relative(q):
        return sum((q >> k & 1) << bit for k, bit in enumerate(bits))

    size = pack1.shape[-1]
    parked = step == 0
    slots, height, count = len(sources), size // chips, chips // 2
    rows = size // 2
    near = [part for block in sources for part in block] + [pack1, pack0]

    def body(place, *refs):
        halves, pack, own_pack, refs = refs[: 2 * slots], refs[2 * slots], refs[2 * slots + 1], refs[2 * slots + 2 :]
        stay, gone, inner, kept, sem = refs
        core, odd, i, z = place[0], place[1], place[2], place[3]
        sector = step * odd + (1 - step) * (1 - odd)
        flags = pack[pl.ds(4 * size, 16), pl.ds(0, 128)].astype(jnp.float32)
        shift1, live1 = (jnp.max(part).astype(jnp.int32) for part in (flags[:8], flags[8:]))
        slot_of, weight_of = [], []
        for shift, live in ((place[4], place[5]), (shift1, live1)):
            rel = sector - shift
            at = step - (2 * odd - 1) * shift
            came = jnp.where(at == 2, 2, at + 2) if step == 0 else jnp.where(at >= 2, at - 1, at + 1)
            slot_of.append(jnp.where((at == 0) | (at == 1), at + 3, came))
            there = ((rel >= 0) | (i > 0)) & ((rel <= 1) | (i < secs - 1))
            weight_of.append(jnp.where(there, live, 0).astype(jnp.float32))

        order = [relative(q) for q in [*range(1, chips, 2), *range(0, chips, 2)]]
        for term in (1, 0):
            def left_rows(group, column, term=term):
                def at(r, k):
                    start = (z ^ r) * height + (core ^ k) * (height // 2)
                    start = start + sector * size
                    block = pl.ds(pl.multiple_of(start, height // 2), height // 2)
                    columns = pl.ds(pl.multiple_of(column * rows, 128), rows)
                    return (own_pack, pack)[term][block, columns]

                return jnp.concatenate([at(r, k) for r in order[group * count : (group + 1) * count] for k in range(2)])

            def first_product(reads, columns, term=term, left_rows=left_rows):
                for group in range(2):
                    product = sum(
                        jnp.dot(left_rows(group, column), read(), preferred_element_type=jnp.float32)
                        for read, column in zip(reads, columns, strict=True)
                    )
                    inner[term, pl.ds(group * rows, rows)] = product.astype(jnp.bfloat16)

            for k in range(slots):
                @pl.when(slot_of[term] == k)
                def _(k=k):
                    parity = z % 2 if swapped[k] else 0
                    first_product([lambda n=n: halves[2 * k + n][...] for n in range(2)], [parity, 1 - parity])

        stay_copy = pltpu.make_async_copy(kept, stay, sem) if parked else None
        for group in (1, 0):
            total = sum(
                lax.dot_general(
                    inner[term, pl.ds(group * rows, rows)],
                    (own_pack, pack)[term][pl.ds(pl.multiple_of((2 + sector) * size, size), size)],
                    (((1,), (1,)), ((), ())),
                    preferred_element_type=jnp.float32,
                )
                * weight_of[term]
                for term in (1, 0)
            )
            for n in range(count):
                block = total[n * height : (n + 1) * height]
                if group == 0:
                    gone[n] = block.astype(gone.dtype)
                else:
                    (kept if parked else stay)[n] = block
            if group == 1 and parked:
                stay_copy.start()
        if parked:
            stay_copy.wait()

    stay_shape = (count, height, size)
    outs = [pltpu.HBM(stay_shape, jnp.float32) if parked else pltpu.VMEM(stay_shape, jnp.float32)]
    outs.append(pltpu.VMEM(stay_shape, jnp.bfloat16))
    return call(
        body,
        "piece",
        out_shape=outs,
        in_specs=[SMEM_SPEC] + [VMEM_SPEC] * len(near),
        out_specs=[ANY_SPEC if parked else VMEM_SPEC] + [VMEM_SPEC] * (len(outs) - 1),
        scratch_shapes=[
            pltpu.VMEM((2, size, size), jnp.bfloat16),
            pltpu.VMEM((count, height, size), jnp.float32),
            pltpu.SemaphoreType.DMA,
        ],
    )(*scalars, *[in_vmem(x) for x in near])


def sum_over_chips(stay, gone, bits, terms, direct):
    half = stay.shape[1] // 2
    cores = [(d, d ^ 1) for d in range(terms)]
    for n, bit in enumerate(bits):
        pairs = [(d, d ^ (2 << bit)) for d in range(terms)]
        if direct and n == len(bits) - 1:
            across = [(d, d ^ (2 << bit) ^ 1) for d in range(terms)]
            swapped = lax.ppermute(stay[0], "term", cores)[half:]
            mine = stay[0, :half] + lax.ppermute(gone[0, :half], "term", pairs).astype(jnp.float32)
            others = swapped + lax.ppermute(gone[0, half:], "term", across).astype(jnp.float32)
            return mine.astype(jnp.bfloat16), others.astype(jnp.bfloat16)
        total = stay + lax.ppermute(gone, "term", pairs).astype(jnp.float32)
        stay, gone = total[::2], total[1::2].astype(jnp.bfloat16)
    total = stay[0].astype(jnp.bfloat16)
    return total[:half], lax.ppermute(total[half:], "term", cores)


def local(psi, left_ops, right_ops, shift, live):
    secs, terms = lax.axis_size("sec"), lax.axis_size("term")
    size = psi.shape[-1]
    i, term = lax.axis_index("sec"), lax.axis_index("term")
    core, odd, z = term % 2, i % 2, term // 2
    cores = [(d, d ^ 1) for d in range(terms)]
    pairs = [(d, d ^ 1) for d in range(secs)]

    place = jnp.stack([core, odd, i, z, shift[0], live[0]]).astype(jnp.int32)
    (*parts, rest), pack0 = cut(place, psi, left_ops, right_ops)
    near = [lax.ppermute(part, "sec", pairs) for part in parts]
    pack1 = lax.ppermute(pack0, "term", cores)
    if secs == 4:
        turn = [(d, d ^ 2) for d in range(secs)]
        far = [lax.ppermute(part, "sec", turn) for part in near[:2]]
        far.append(lax.ppermute(copy_after(near[2], far[0]), "sec", turn))
    else:
        nexts = [(d, d + 1) for d in range(1, secs - 1, 2)]
        nexts = nexts + [(b, a) for a, b in nexts]
        far = [lax.ppermute(part, "sec", nexts) for part in parts]
    planes = [(d, d ^ 2) for d in range(terms)]
    near_first, near_second = (near[0], lax.ppermute(near[0], "term", planes)), near[1:]
    far_first, far_second = (far[0], lax.ppermute(copy_after(far[0], near[1], near_first[1]), "term", planes)), far[1:]

    scalars = (place,)
    outs = []
    for step in range(2):
        came = (near_first, near_second, far_first) if step == 0 else (near_second, far_first, far_second)
        sources = (*came, parts[1:], (parts[0], rest))
        swapped = (True, False, True, False, True) if step == 0 else (False, True, False, False, True)
        bits = list(range((terms // 2).bit_length() - 1))
        blocks = piece(step, secs, terms // 2, bits, scalars, sources, swapped, pack1, pack0)
        mine, got = sum_over_chips(*blocks, bits, terms, step == 1)
        outs.append(jnp.where(core == 0, jnp.stack([mine, got]), jnp.stack([got, mine])))
    return jnp.where(odd == 1, jnp.stack(outs), jnp.stack(outs[::-1]))


def solution(mesh):
    in_specs = (
        P("sec", None, None, None),
        P("term", "sec", None, None),
        P("term", "sec", None, None),
        P("term"),
        P("term"),
    )
    out_specs = P("sec", None, "term", None)
    return jax.shard_map(local, mesh=mesh, in_specs=in_specs, out_specs=out_specs, check_vma=False)
```

```python
import jax
import jax.numpy as jnp
from jax import lax
from jax.experimental import pallas as pl
from jax.experimental.pallas import tpu as pltpu
from jax.sharding import PartitionSpec as P

DQ = 2
VMEM_LIMIT = 12 * 1024 * 1024
SMEM_SPEC = pl.BlockSpec(memory_space=pltpu.SMEM)
VMEM_SPEC = pl.BlockSpec(memory_space=pltpu.VMEM)
ANY_SPEC = pl.BlockSpec(memory_space=pl.ANY)


def in_vmem(array):
    return pltpu.with_memory_space_constraint(array, pltpu.VMEM)


def in_hbm(array):
    return pltpu.with_memory_space_constraint(array, pltpu.HBM)


def call(body, name, **kwargs):
    return pl.pallas_call(
        body,
        compiler_params=pltpu.CompilerParams(vmem_limit_bytes=VMEM_LIMIT),
        cost_estimate=pl.CostEstimate(flops=1000, bytes_accessed=1000, transcendentals=0),
        name=name,
        **kwargs,
    )


def cut(place, psi, left, right):
    size = psi.shape[-1]
    rows = size // 2

    def body(place_ref, psi_ref, left_ref, right_ref, *refs):
        parts, pack, sem = refs[:4], refs[4], refs[5]
        core, odd, half = place_ref[0], place_ref[1], place_ref[3] % 2
        copies = [
            pltpu.make_async_copy(psi_ref.at[sector, core, pl.ds(start * rows, rows)], part, sem.at[n])
            for n, (part, sector, start) in enumerate(zip(parts, (odd, 1 - odd, 1 - odd, odd), (half, 0, 1, 1 - half), strict=True))
        ]
        for k, ref in enumerate((left_ref, right_ref)):
            for s in range(2):
                at = pl.ds((2 * k + s) * size, size)
                copies.append(pltpu.make_async_copy(ref.at[0, s], pack.at[at], sem.at[4 + 2 * k + s]))
        for copy in copies:
            copy.start()
        number = lax.broadcasted_iota(jnp.int32, (16, size), 0)
        flags = jnp.where(number < 8, place_ref[4], place_ref[5])
        pack[pl.ds(4 * size, 16)] = flags.astype(jnp.float32).astype(pack.dtype)
        for copy in copies:
            copy.wait()

    out = [pltpu.VMEM((rows, size), psi.dtype)] * 4 + [pltpu.VMEM((4 * size + 16, size), psi.dtype)]
    *parts, pack = call(
        body,
        "cut",
        out_shape=out,
        in_specs=[SMEM_SPEC] + [ANY_SPEC] * 3,
        out_specs=[VMEM_SPEC] * 5,
        scratch_shapes=[pltpu.SemaphoreType.DMA((8,))],
    )(place, in_hbm(psi), in_hbm(left), in_hbm(right))
    return parts, pack


def copy_after(part, *after):
    def body(part_ref, *refs):
        out, sem = refs[-2:]
        copy = pltpu.make_async_copy(part_ref, out, sem)
        copy.start()
        copy.wait()

    return call(
        body,
        "copy_after",
        out_shape=pltpu.VMEM(part.shape, part.dtype),
        in_specs=[VMEM_SPEC] + [ANY_SPEC] * len(after),
        out_specs=VMEM_SPEC,
        scratch_shapes=[pltpu.SemaphoreType.DMA],
    )(in_vmem(part), *after)


def piece(step, secs, chips, bits, scalars, sources, swapped, pack1, pack0):
    def relative(q):
        return sum((q >> k & 1) << bit for k, bit in enumerate(bits))

    size = pack1.shape[-1]
    parked = step == 0
    slots, height, count = len(sources), size // chips, chips // 2
    rows = size // 2
    near = [part for block in sources for part in block] + [pack1, pack0]

    def body(place, *refs):
        halves, pack, own_pack, refs = refs[: 2 * slots], refs[2 * slots], refs[2 * slots + 1], refs[2 * slots + 2 :]
        stay, gone, inner, kept, sem = refs
        core, odd, i, z = place[0], place[1], place[2], place[3]
        sector = step * odd + (1 - step) * (1 - odd)
        flags = pack[pl.ds(4 * size, 16), pl.ds(0, 128)].astype(jnp.float32)
        shift1, live1 = (jnp.max(part).astype(jnp.int32) for part in (flags[:8], flags[8:]))
        slot_of, weight_of = [], []
        for shift, live in ((place[4], place[5]), (shift1, live1)):
            rel = sector - shift
            at = step - (2 * odd - 1) * shift
            came = jnp.where(at == 2, 2, at + 2) if step == 0 else jnp.where(at >= 2, at - 1, at + 1)
            slot_of.append(jnp.where((at == 0) | (at == 1), at + 3, came))
            there = ((rel >= 0) | (i > 0)) & ((rel <= 1) | (i < secs - 1))
            weight_of.append(jnp.where(there, live, 0).astype(jnp.float32))

        order = [relative(q) for q in [*range(1, chips, 2), *range(0, chips, 2)]]
        for term in (1, 0):
            def left_rows(group, column, term=term):
                def at(r, k):
                    start = (z ^ r) * height + (core ^ k) * (height // 2)
                    start = start + sector * size
                    block = pl.ds(pl.multiple_of(start, height // 2), height // 2)
                    columns = pl.ds(pl.multiple_of(column * rows, 128), rows)
                    return (own_pack, pack)[term][block, columns]

                return jnp.concatenate([at(r, k) for r in order[group * count : (group + 1) * count] for k in range(2)])

            def first_product(reads, columns, term=term, left_rows=left_rows):
                for group in range(2):
                    product = sum(
                        jnp.dot(left_rows(group, column), read(), preferred_element_type=jnp.float32)
                        for read, column in zip(reads, columns, strict=True)
                    )
                    inner[term, pl.ds(group * rows, rows)] = product.astype(jnp.bfloat16)

            for k in range(slots):
                @pl.when(slot_of[term] == k)
                def _(k=k):
                    parity = z % 2 if swapped[k] else 0
                    first_product([lambda n=n: halves[2 * k + n][...] for n in range(2)], [parity, 1 - parity])

        stay_copy = pltpu.make_async_copy(kept, stay, sem) if parked else None
        for group in (1, 0):
            total = sum(
                lax.dot_general(
                    inner[term, pl.ds(group * rows, rows)],
                    (own_pack, pack)[term][pl.ds(pl.multiple_of((2 + sector) * size, size), size)],
                    (((1,), (1,)), ((), ())),
                    preferred_element_type=jnp.float32,
                )
                * weight_of[term]
                for term in (1, 0)
            )
            for n in range(count):
                block = total[n * height : (n + 1) * height]
                if group == 0:
                    gone[n] = block.astype(gone.dtype)
                else:
                    (kept if parked else stay)[n] = block
            if group == 1 and parked:
                stay_copy.start()
        if parked:
            stay_copy.wait()

    stay_shape = (count, height, size)
    outs = [pltpu.HBM(stay_shape, jnp.float32) if parked else pltpu.VMEM(stay_shape, jnp.float32)]
    outs.append(pltpu.VMEM(stay_shape, jnp.bfloat16))
    return call(
        body,
        "piece",
        out_shape=outs,
        in_specs=[SMEM_SPEC] + [VMEM_SPEC] * len(near),
        out_specs=[ANY_SPEC if parked else VMEM_SPEC] + [VMEM_SPEC] * (len(outs) - 1),
        scratch_shapes=[
            pltpu.VMEM((2, size, size), jnp.bfloat16),
            pltpu.VMEM((count, height, size), jnp.float32),
            pltpu.SemaphoreType.DMA,
        ],
    )(*scalars, *[in_vmem(x) for x in near])


def sum_over_chips(stay, gone, bits, terms, direct):
    half = stay.shape[1] // 2
    cores = [(d, d ^ 1) for d in range(terms)]
    for n, bit in enumerate(bits):
        pairs = [(d, d ^ (2 << bit)) for d in range(terms)]
        if direct and n == len(bits) - 1:
            across = [(d, d ^ (2 << bit) ^ 1) for d in range(terms)]
            swapped = lax.ppermute(stay[0], "term", cores)[half:]
            mine = stay[0, :half] + lax.ppermute(gone[0, :half], "term", pairs).astype(jnp.float32)
            others = swapped + lax.ppermute(gone[0, half:], "term", across).astype(jnp.float32)
            return mine.astype(jnp.bfloat16), others.astype(jnp.bfloat16)
        total = stay + lax.ppermute(gone, "term", pairs).astype(jnp.float32)
        stay, gone = total[::2], total[1::2].astype(jnp.bfloat16)
    total = stay[0].astype(jnp.bfloat16)
    return total[:half], lax.ppermute(total[half:], "term", cores)


def local(psi, left_ops, right_ops, shift, live):
    secs, terms = lax.axis_size("sec"), lax.axis_size("term")
    size = psi.shape[-1]
    i, term = lax.axis_index("sec"), lax.axis_index("term")
    core, odd, z = term % 2, i % 2, term // 2
    cores = [(d, d ^ 1) for d in range(terms)]
    pairs = [(d, d ^ 1) for d in range(secs)]

    place = jnp.stack([core, odd, i, z, shift[0], live[0]]).astype(jnp.int32)
    (*parts, rest), pack0 = cut(place, psi, left_ops, right_ops)
    near = [lax.ppermute(part, "sec", pairs) for part in parts]
    pack1 = lax.ppermute(pack0, "term", cores)
    if secs == 4:
        turn = [(d, d ^ 2) for d in range(secs)]
        far = [lax.ppermute(part, "sec", turn) for part in near[:2]]
        far.append(lax.ppermute(copy_after(near[2], far[0]), "sec", turn))
    else:
        nexts = [(d, d + 1) for d in range(1, secs - 1, 2)]
        nexts = nexts + [(b, a) for a, b in nexts]
        far = [lax.ppermute(part, "sec", nexts) for part in parts]
    planes = [(d, d ^ 2) for d in range(terms)]
    near_first, near_second = (near[0], lax.ppermute(near[0], "term", planes)), near[1:]
    far_first, far_second = (far[0], lax.ppermute(copy_after(far[0], near[1]), "term", planes)), far[1:]

    scalars = (place,)
    outs = []
    for step in range(2):
        came = (near_first, near_second, far_first) if step == 0 else (near_second, far_first, far_second)
        sources = (*came, parts[1:], (parts[0], rest))
        swapped = (True, False, True, False, True) if step == 0 else (False, True, False, False, True)
        bits = list(range((terms // 2).bit_length() - 1))
        blocks = piece(step, secs, terms // 2, bits, scalars, sources, swapped, pack1, pack0)
        mine, got = sum_over_chips(*blocks, bits, terms, step == 1)
        outs.append(jnp.where(core == 0, jnp.stack([mine, got]), jnp.stack([got, mine])))
    return jnp.where(odd == 1, jnp.stack(outs), jnp.stack(outs[::-1]))


def solution(mesh):
    in_specs = (
        P("sec", None, None, None),
        P("term", "sec", None, None),
        P("term", "sec", None, None),
        P("term"),
        P("term"),
    )
    out_specs = P("sec", None, "term", None)
    return jax.shard_map(local, mesh=mesh, in_specs=in_specs, out_specs=out_specs, check_vma=False)
```

```python
import jax
import jax.numpy as jnp
from jax import lax
from jax.experimental import pallas as pl
from jax.experimental.pallas import tpu as pltpu
from jax.sharding import PartitionSpec as P

DQ = 2
VMEM_LIMIT = 12 * 1024 * 1024
SMEM_SPEC = pl.BlockSpec(memory_space=pltpu.SMEM)
VMEM_SPEC = pl.BlockSpec(memory_space=pltpu.VMEM)
ANY_SPEC = pl.BlockSpec(memory_space=pl.ANY)


def in_vmem(array):
    return pltpu.with_memory_space_constraint(array, pltpu.VMEM)


def in_hbm(array):
    return pltpu.with_memory_space_constraint(array, pltpu.HBM)


def call(body, name, **kwargs):
    return pl.pallas_call(
        body,
        compiler_params=pltpu.CompilerParams(vmem_limit_bytes=VMEM_LIMIT),
        cost_estimate=pl.CostEstimate(flops=1000, bytes_accessed=1000, transcendentals=0),
        name=name,
        **kwargs,
    )


def cut(place, psi, left, right):
    size = psi.shape[-1]
    rows = size // 2

    def body(place_ref, psi_ref, left_ref, right_ref, *refs):
        parts, pack, sem = refs[:4], refs[4], refs[5]
        core, odd, half = place_ref[0], place_ref[1], place_ref[3] % 2
        copies = [
            pltpu.make_async_copy(psi_ref.at[sector, core, pl.ds(start * rows, rows)], part, sem.at[n])
            for n, (part, sector, start) in enumerate(zip(parts, (odd, 1 - odd, 1 - odd, odd), (half, 0, 1, 1 - half), strict=True))
        ]
        for k, ref in enumerate((left_ref, right_ref)):
            for s in range(2):
                at = pl.ds((2 * k + s) * size, size)
                copies.append(pltpu.make_async_copy(ref.at[0, s], pack.at[at], sem.at[4 + 2 * k + s]))
        for copy in copies:
            copy.start()
        number = lax.broadcasted_iota(jnp.int32, (16, size), 0)
        flags = jnp.where(number < 8, place_ref[4], place_ref[5])
        pack[pl.ds(4 * size, 16)] = flags.astype(jnp.float32).astype(pack.dtype)
        for copy in copies:
            copy.wait()

    out = [pltpu.VMEM((rows, size), psi.dtype)] * 4 + [pltpu.VMEM((4 * size + 16, size), psi.dtype)]
    *parts, pack = call(
        body,
        "cut",
        out_shape=out,
        in_specs=[SMEM_SPEC] + [ANY_SPEC] * 3,
        out_specs=[VMEM_SPEC] * 5,
        scratch_shapes=[pltpu.SemaphoreType.DMA((8,))],
    )(place, in_hbm(psi), in_hbm(left), in_hbm(right))
    return parts, pack


def copy_after(part, *after):
    def body(part_ref, *refs):
        out, sem = refs[-2:]
        copy = pltpu.make_async_copy(part_ref, out, sem)
        copy.start()
        copy.wait()

    return call(
        body,
        "copy_after",
        out_shape=pltpu.VMEM(part.shape, part.dtype),
        in_specs=[VMEM_SPEC] + [ANY_SPEC] * len(after),
        out_specs=VMEM_SPEC,
        scratch_shapes=[pltpu.SemaphoreType.DMA],
    )(in_vmem(part), *after)


def piece(step, secs, chips, bits, scalars, sources, swapped, pack1, pack0):
    def relative(q):
        return sum((q >> k & 1) << bit for k, bit in enumerate(bits))

    size = pack1.shape[-1]
    parked = step == 0
    slots, height, count = len(sources), size // chips, chips // 2
    rows = size // 2
    near = [part for block in sources for part in block] + [pack1, pack0]

    def body(place, *refs):
        halves, pack, own_pack, refs = refs[: 2 * slots], refs[2 * slots], refs[2 * slots + 1], refs[2 * slots + 2 :]
        stay, gone, inner, kept, sem = refs
        core, odd, i, z = place[0], place[1], place[2], place[3]
        sector = step * odd + (1 - step) * (1 - odd)
        flags = pack[pl.ds(4 * size, 16), pl.ds(0, 128)].astype(jnp.float32)
        shift1, live1 = (jnp.max(part).astype(jnp.int32) for part in (flags[:8], flags[8:]))
        slot_of, weight_of = [], []
        for shift, live in ((place[4], place[5]), (shift1, live1)):
            rel = sector - shift
            at = step - (2 * odd - 1) * shift
            came = jnp.where(at == 2, 2, at + 2) if step == 0 else jnp.where(at >= 2, at - 1, at + 1)
            slot_of.append(jnp.where((at == 0) | (at == 1), at + 3, came))
            there = ((rel >= 0) | (i > 0)) & ((rel <= 1) | (i < secs - 1))
            weight_of.append(jnp.where(there, live, 0).astype(jnp.float32))

        order = [relative(q) for q in [*range(1, chips, 2), *range(0, chips, 2)]]
        for term in (1, 0):
            def left_rows(group, column, term=term):
                def at(r, k):
                    start = (z ^ r) * height + (core ^ k) * (height // 2)
                    start = start + sector * size
                    block = pl.ds(pl.multiple_of(start, height // 2), height // 2)
                    columns = pl.ds(pl.multiple_of(column * rows, 128), rows)
                    return (own_pack, pack)[term][block, columns]

                return jnp.concatenate([at(r, k) for r in order[group * count : (group + 1) * count] for k in range(2)])

            def first_product(reads, columns, term=term, left_rows=left_rows):
                for group in range(2):
                    product = sum(
                        jnp.dot(left_rows(group, column), read(), preferred_element_type=jnp.float32)
                        for read, column in zip(reads, columns, strict=True)
                    )
                    inner[term, pl.ds(group * rows, rows)] = product.astype(jnp.bfloat16)

            for k in range(slots):
                @pl.when(slot_of[term] == k)
                def _(k=k):
                    parity = z % 2 if swapped[k] else 0
                    first_product([lambda n=n: halves[2 * k + n][...] for n in range(2)], [parity, 1 - parity])

        stay_copy = pltpu.make_async_copy(kept, stay, sem) if parked else None
        for group in (1, 0):
            total = sum(
                lax.dot_general(
                    inner[term, pl.ds(group * rows, rows)],
                    (own_pack, pack)[term][pl.ds(pl.multiple_of((2 + sector) * size, size), size)],
                    (((1,), (1,)), ((), ())),
                    preferred_element_type=jnp.float32,
                )
                * weight_of[term]
                for term in (1, 0)
            )
            for n in range(count):
                block = total[n * height : (n + 1) * height]
                if group == 0:
                    gone[n] = block.astype(gone.dtype)
                else:
                    (kept if parked else stay)[n] = block
            if group == 1 and parked:
                stay_copy.start()
        if parked:
            stay_copy.wait()

    stay_shape = (count, height, size)
    outs = [pltpu.HBM(stay_shape, jnp.float32) if parked else pltpu.VMEM(stay_shape, jnp.float32)]
    outs.append(pltpu.VMEM(stay_shape, jnp.bfloat16))
    return call(
        body,
        "piece",
        out_shape=outs,
        in_specs=[SMEM_SPEC] + [VMEM_SPEC] * len(near),
        out_specs=[ANY_SPEC if parked else VMEM_SPEC] + [VMEM_SPEC] * (len(outs) - 1),
        scratch_shapes=[
            pltpu.VMEM((2, size, size), jnp.bfloat16),
            pltpu.VMEM((count, height, size), jnp.float32),
            pltpu.SemaphoreType.DMA,
        ],
    )(*scalars, *[in_vmem(x) for x in near])


def sum_over_chips(stay, gone, bits, terms, direct):
    half = stay.shape[1] // 2
    cores = [(d, d ^ 1) for d in range(terms)]
    for n, bit in enumerate(bits):
        pairs = [(d, d ^ (2 << bit)) for d in range(terms)]
        if direct and n == len(bits) - 1:
            across = [(d, d ^ (2 << bit) ^ 1) for d in range(terms)]
            swapped = lax.ppermute(stay[0], "term", cores)[half:]
            others = swapped + lax.ppermute(gone[0, half:], "term", across).astype(jnp.float32)
            mine = stay[0, :half] + lax.ppermute(gone[0, :half], "term", pairs).astype(jnp.float32)
            return mine.astype(jnp.bfloat16), others.astype(jnp.bfloat16)
        total = stay + lax.ppermute(gone, "term", pairs).astype(jnp.float32)
        stay, gone = total[::2], total[1::2].astype(jnp.bfloat16)
    total = stay[0].astype(jnp.bfloat16)
    return total[:half], lax.ppermute(total[half:], "term", cores)


def local(psi, left_ops, right_ops, shift, live):
    secs, terms = lax.axis_size("sec"), lax.axis_size("term")
    size = psi.shape[-1]
    i, term = lax.axis_index("sec"), lax.axis_index("term")
    core, odd, z = term % 2, i % 2, term // 2
    cores = [(d, d ^ 1) for d in range(terms)]
    pairs = [(d, d ^ 1) for d in range(secs)]

    place = jnp.stack([core, odd, i, z, shift[0], live[0]]).astype(jnp.int32)
    (*parts, rest), pack0 = cut(place, psi, left_ops, right_ops)
    near = [lax.ppermute(part, "sec", pairs) for part in parts]
    pack1 = lax.ppermute(pack0, "term", cores)
    if secs == 4:
        turn = [(d, d ^ 2) for d in range(secs)]
        far = [lax.ppermute(part, "sec", turn) for part in near[:2]]
        far.append(lax.ppermute(copy_after(near[2], far[0]), "sec", turn))
    else:
        nexts = [(d, d + 1) for d in range(1, secs - 1, 2)]
        nexts = nexts + [(b, a) for a, b in nexts]
        far = [lax.ppermute(part, "sec", nexts) for part in parts]
    planes = [(d, d ^ 2) for d in range(terms)]
    near_first, near_second = (near[0], lax.ppermute(near[0], "term", planes)), near[1:]
    far_first, far_second = (far[0], lax.ppermute(copy_after(far[0], near[1], pack1), "term", planes)), far[1:]

    scalars = (place,)
    outs = []
    for step in range(2):
        came = (near_first, near_second, far_first) if step == 0 else (near_second, far_first, far_second)
        sources = (*came, parts[1:], (parts[0], rest))
        swapped = (True, False, True, False, True) if step == 0 else (False, True, False, False, True)
        bits = list(range((terms // 2).bit_length() - 1))
        blocks = piece(step, secs, terms // 2, bits, scalars, sources, swapped, pack1, pack0)
        mine, got = sum_over_chips(*blocks, bits, terms, step == 1)
        outs.append(jnp.where(core == 0, jnp.stack([mine, got]), jnp.stack([got, mine])))
    return jnp.where(odd == 1, jnp.stack(outs), jnp.stack(outs[::-1]))


def solution(mesh):
    in_specs = (
        P("sec", None, None, None),
        P("term", "sec", None, None),
        P("term", "sec", None, None),
        P("term"),
        P("term"),
    )
    out_specs = P("sec", None, "term", None)
    return jax.shard_map(local, mesh=mesh, in_specs=in_specs, out_specs=out_specs, check_vma=False)
```
